32 devices in a mesh: section: 4 (over y, x), tok: 8 (over z, core).
Axes of the slice: x: 2, y: 2, z: 4, core: 2. Of those that a mesh axis runs over, the one named last changes fastest.
Arguments:
- tokens: bfloat16 [2, 1024, 768], P(None, 'tok'), may hold values from -6 to 6
- cotangent: bfloat16 [2, 1024, 768], P(None, 'tok'), may hold values from -0.13183594 to 0.13183594
- window_slot: int32 [1024], P('tok'), may hold values from 0 to 1023, as said below
- slot_token: int32 [1024], P('tok'), may hold values from 0 to 1023, as said below
- norm_gain: float32 [4, 768], P('section'), may hold values from 0.25 to 1.75
- qkv_weight: bfloat16 [4, 768, 2304], P('section')
- out_weight: bfloat16 [4, 768, 768], P('section'), may hold values from -0.21875 to 0.21875
Outputs:
- grad_qkv: float32 [4, 768, 2304], P('section', 'tok')
- grad_out: float32 [4, 768, 768], P('section', 'tok')
- grad_gain: float32 [4, 768], P('section', 'tok')
The draws below stay inside these ranges and needn't reach their ends.
Inputs may be any that keep to these rules, and one draw needn't show every extreme that they name: window_slot and slot_token are inverse permutations: slot_token[window_slot[t]] = t. Slots k * 128 .. (k + 1) * 128 - 1 lie on the k-th device of tok, and the tokens of every device fill exactly 16 slots of every device. `slot_token`: the inverse permutation of window_slot.
All inputs are finite; a program needn't handle non-finite values.
Results may differ from the reference program's by a relative error of at most 0.025.
Values may be sent and summed in bfloat16 or wider, within the bound.
A program may use at most 128 MiB of HBM per device.

```python
import jax
import jax.numpy as jnp
from jax import lax

D = 768
HEADS = 12
WINDOW = 32
TOK_DEV = 128
MICRO = 2
SECTIONS = 4
TOKENS = 1024
PEER_ROWS = 16
N_TOK = 8


def slot_tables(key):
    base_key = jax.random.fold_in(key, 7)
    source_keys = jax.random.split(jax.random.fold_in(base_key, 1), N_TOK)
    target_keys = jax.random.split(jax.random.fold_in(base_key, 2), N_TOK)
    source_order = jax.vmap(lambda item_key: jax.random.permutation(item_key, TOK_DEV))(source_keys).astype(jnp.int32)
    target_order = jax.vmap(lambda item_key: jax.random.permutation(item_key, TOK_DEV))(target_keys).astype(jnp.int32)
    device = jnp.arange(N_TOK, dtype=jnp.int32)[:, None]
    rank_local = jnp.arange(TOK_DEV, dtype=jnp.int32)[None, :]
    token_ids = device * TOK_DEV + source_order
    target = rank_local // PEER_ROWS
    incoming = device * PEER_ROWS + rank_local % PEER_ROWS
    slot_ids = target * TOK_DEV + target_order[target, incoming]
    window_table = jnp.zeros((TOKENS,), jnp.int32).at[token_ids.reshape(-1)].set(slot_ids.reshape(-1))
    token_table = jnp.zeros((TOKENS,), jnp.int32).at[slot_ids.reshape(-1)].set(token_ids.reshape(-1))
    return (window_table, token_table)


def draw_window_slot(key, part):
    return slot_tables(key)[0]


def draw_slot_token(key, part):
    return slot_tables(key)[1]


def draw_qkv_weight(key, part):
    base_weight = jax.random.normal(jax.random.fold_in(key, 1), (SECTIONS, D, 3 * D), jnp.float32) * D ** (-0.5)
    return base_weight.astype(jnp.bfloat16)


def level_of(stream_key, shape, cuts, least, high):
    loudness, own = 1.0, jax.random.fold_in(stream_key, 6)
    for axis_at, parts in cuts:
        steps = jnp.exp(jax.random.uniform(jax.random.fold_in(own, axis_at), (parts,), jnp.float32, least / len(cuts), high / len(cuts)))
        loudness = loudness * jnp.repeat(steps, shape[axis_at] // parts).reshape([-1 if axis == axis_at else 1 for axis in range(len(shape))])
    return loudness


def noise(rng, shape, spread, most, pieces=(), kind=jnp.bfloat16):
    level = level_of(rng, shape, pieces, -0.22, 0.18) if pieces else 1.0
    drawn = jax.random.normal(rng, shape, jnp.float32) * spread * level
    return jnp.minimum(jnp.maximum(drawn, -most), most).astype(kind)


def setup_inputs(seed: int = 0) -> dict:
    streams_of = jax.random.split(jax.random.key(seed), 8)
    tokens = noise(streams_of[0], (MICRO, TOKENS, D), 1.0, 6.0, ((1, 8),))
    cotangent = noise(streams_of[1], (MICRO, TOKENS, D), ((MICRO * TOKENS) ** -0.5), 0.13183594, ((1, 8),))
    window_slot = draw_window_slot(jax.random.fold_in(streams_of[7], 71), 0)
    slot_token = draw_slot_token(jax.random.fold_in(streams_of[7], 71), 0)
    norm_gain = jnp.clip(1.0 + 0.15 * jax.random.normal(streams_of[4], (SECTIONS, D), jnp.float32), 0.25, 1.75)
    qkv_weight = draw_qkv_weight(jax.random.fold_in(streams_of[7], 71), 0)
    out_weight = noise(streams_of[6], (SECTIONS, D, D), D ** -0.5, 0.21875, ((0, 4),))
    return {"tokens": tokens, "cotangent": cotangent, "window_slot": window_slot, "slot_token": slot_token, "norm_gain": norm_gain, "qkv_weight": qkv_weight, "out_weight": out_weight}


EPSILON = 1e-06

def normalize(rows_in, norm_scale):
    widened = rows_in.astype(jnp.float32)
    factor = lax.rsqrt(lax.optimization_barrier(jnp.mean(widened * widened, axis=-1, keepdims=True)) + EPSILON)
    return ((widened * factor * norm_scale).astype(jnp.bfloat16), factor)

def window_split(window_rows):
    row_total = window_rows.shape[0]
    head_dim = window_rows.shape[1] // 3 // HEADS
    shaped = window_rows.astype(jnp.float32).reshape(row_total // WINDOW, WINDOW, 3, HEADS, head_dim)
    return (shaped[:, :, 0], shaped[:, :, 1], shaped[:, :, 2], head_dim)

def window_soft(queries, key_rows, head_dim):
    scores = jnp.einsum('wqhd,wkhd->whqk', queries, key_rows) * head_dim ** (-0.5)
    return jax.nn.softmax(scores, axis=-1)

def rounded(array_in):
    return lax.optimization_barrier(array_in.astype(jnp.bfloat16)).astype(jnp.float32)

def window_forward(window_rows):
    queries, key_rows, values, head_dim = window_split(window_rows)
    soft_weights = rounded(window_soft(queries, key_rows, head_dim))
    mixed_rows = jnp.einsum('whqk,wkhd->wqhd', soft_weights, values)
    return mixed_rows.reshape(window_rows.shape[0], -1).astype(jnp.bfloat16)

def window_backward(window_rows, grad_rows):
    queries, key_rows, values, head_dim = window_split(window_rows)
    row_total = window_rows.shape[0]
    grad_mixed = grad_rows.astype(jnp.float32).reshape(row_total // WINDOW, WINDOW, HEADS, head_dim)
    soft_weights = window_soft(queries, key_rows, head_dim)
    soft_low = rounded(soft_weights)
    grad_soft = jnp.einsum('wqhd,wkhd->whqk', grad_mixed, values)
    grad_values = jnp.einsum('whqk,wqhd->wkhd', soft_low, grad_mixed)
    grad_scores = soft_weights * (grad_soft - lax.optimization_barrier(jnp.sum(soft_weights * grad_soft, axis=-1, keepdims=True)))
    grad_low = rounded(grad_scores)
    temper = head_dim ** (-0.5)
    grad_queries = jnp.einsum('whqk,wkhd->wqhd', grad_low, key_rows) * temper
    grad_keys = jnp.einsum('whqk,wqhd->wkhd', grad_low, queries) * temper
    stacked = jnp.stack([grad_queries, grad_keys, grad_values], axis=2)
    return stacked.reshape(row_total, -1).astype(jnp.bfloat16)

def reference(tokens, cotangent, window_slot, slot_token, norm_gain, qkv_weight, out_weight):
    section_count = qkv_weight.shape[0]
    micro_count = tokens.shape[0]
    slot_index = slot_token.astype(jnp.int32)
    token_index = window_slot.astype(jnp.int32)
    saved = []
    for micro_index in range(micro_count):
        layer_in = tokens[micro_index]
        per_section = []
        for section_index in range(section_count):
            normed, factor = normalize(layer_in, norm_gain[section_index])
            projected = jnp.dot(normed, qkv_weight[section_index], preferred_element_type=jnp.float32).astype(jnp.bfloat16)
            window_rows = jnp.take(projected, slot_index, axis=0)
            mixed_rows = jnp.take(window_forward(window_rows), token_index, axis=0)
            layer_out = (layer_in.astype(jnp.float32) + jnp.dot(mixed_rows, out_weight[section_index], preferred_element_type=jnp.float32)).astype(jnp.bfloat16)
            per_section.append((layer_in, normed, factor, window_rows, mixed_rows))
            layer_in = layer_out
        saved.append(per_section)
    qkv_total = jnp.zeros(qkv_weight.shape, jnp.float32)
    out_total = jnp.zeros(out_weight.shape, jnp.float32)
    scale_total = jnp.zeros(norm_gain.shape, jnp.float32)
    for micro_index in range(micro_count):
        grad_layer = cotangent[micro_index]
        for section_index in range(section_count - 1, -1, -1):
            layer_in, normed, factor, window_rows, mixed_rows = saved[micro_index][section_index]
            out_total = out_total.at[section_index].add(jnp.dot(mixed_rows.T, grad_layer, preferred_element_type=jnp.float32))
            grad_mixed = jnp.dot(grad_layer, out_weight[section_index].T, preferred_element_type=jnp.float32).astype(jnp.bfloat16)
            grad_window = window_backward(window_rows, jnp.take(grad_mixed, slot_index, axis=0))
            grad_proj = jnp.take(grad_window, token_index, axis=0)
            qkv_total = qkv_total.at[section_index].add(jnp.dot(normed.T, grad_proj, preferred_element_type=jnp.float32))
            grad_normed = jnp.dot(grad_proj, qkv_weight[section_index].T, preferred_element_type=jnp.float32)
            widened = layer_in.astype(jnp.float32)
            norm_scale = norm_gain[section_index]
            scale_total = scale_total.at[section_index].add(lax.optimization_barrier(jnp.sum(grad_normed * widened * factor, axis=0)))
            scaled = norm_scale * grad_normed
            inner_mean = lax.optimization_barrier(jnp.mean(scaled * widened, axis=-1, keepdims=True))
            grad_layer = (grad_layer.astype(jnp.float32) + factor * scaled - widened * factor ** 3 * inner_mean).astype(jnp.bfloat16)
    return (qkv_total, out_total, scale_total)
```

```python
import jax
import jax.numpy as jnp
from jax import lax
from jax.sharding import PartitionSpec as P

HEADS = 12
WINDOW = 32


EPSILON = 1e-06


def from_behind(value, axis, steps):
    count = lax.axis_size(axis)
    first, last = (max(0, -steps), min(count, count - steps))
    return lax.ppermute(value, axis, [(source, source + steps) for source in range(first, last)])


def normalize(rows_in, norm_scale):
    widened = rows_in.astype(jnp.float32)
    factor = lax.rsqrt(jnp.mean(widened * widened, axis=-1, keepdims=True) + EPSILON)
    return ((widened * factor * norm_scale).astype(jnp.bfloat16), factor)


def window_split(window_rows):
    row_total = window_rows.shape[0]
    head_dim = window_rows.shape[1] // 3 // HEADS
    shaped = window_rows.reshape(row_total // WINDOW, WINDOW, 3, HEADS, head_dim)
    return (shaped[:, :, 0], shaped[:, :, 1], shaped[:, :, 2], head_dim)


def window_soft(queries, key_rows, head_dim):
    scores = jnp.einsum(
        "wqhd,wkhd->whqk", queries, key_rows, preferred_element_type=jnp.float32
    ) * head_dim ** (-0.5)
    return jax.nn.softmax(scores, axis=-1)


def window_forward(window_rows):
    queries, key_rows, values, head_dim = window_split(window_rows)
    soft_weights = window_soft(queries, key_rows, head_dim).astype(jnp.bfloat16)
    mixed_rows = jnp.einsum(
        "whqk,wkhd->wqhd", soft_weights, values, preferred_element_type=jnp.float32
    )
    return mixed_rows.reshape(window_rows.shape[0], -1).astype(jnp.bfloat16)


def window_backward(window_rows, grad_rows):
    queries, key_rows, values, head_dim = window_split(window_rows)
    row_total = window_rows.shape[0]
    grad_mixed = grad_rows.reshape(row_total // WINDOW, WINDOW, HEADS, head_dim)
    soft_weights = window_soft(queries, key_rows, head_dim)
    soft_low = soft_weights.astype(jnp.bfloat16)
    grad_soft = jnp.einsum(
        "wqhd,wkhd->whqk", grad_mixed, values, preferred_element_type=jnp.float32
    )
    grad_values = jnp.einsum(
        "whqk,wqhd->wkhd", soft_low, grad_mixed, preferred_element_type=jnp.float32
    )
    grad_scores = soft_weights * (
        grad_soft - jnp.sum(soft_weights * grad_soft, axis=-1, keepdims=True)
    )
    grad_low = grad_scores.astype(jnp.bfloat16)
    temper = head_dim ** (-0.5)
    grad_queries = (
        jnp.einsum("whqk,wkhd->wqhd", grad_low, key_rows, preferred_element_type=jnp.float32)
        * temper
    )
    grad_keys = (
        jnp.einsum("whqk,wqhd->wkhd", grad_low, queries, preferred_element_type=jnp.float32)
        * temper
    )
    stacked = jnp.stack([grad_queries, grad_keys, grad_values], axis=2)
    return stacked.reshape(row_total, -1).astype(jnp.bfloat16)


def stored_update(stored, position, active, update):
    former = lax.dynamic_index_in_dim(stored, position, 0, keepdims=False)
    return lax.dynamic_update_index_in_dim(stored, jnp.where(active, update, former), position, 0)


def per_device(tokens, cotangent, window_slot, slot_token, norm_gain, qkv_weight, out_weight):
    micro_count, row_count, feature_width = tokens.shape
    section_count = lax.axis_size("section")
    section_index = lax.axis_index("section")
    norm_scale = norm_gain[0]
    qkv_matrix = qkv_weight[0]
    out_matrix = out_weight[0]
    target_device = window_slot // row_count
    send_order = jnp.argsort(target_device, stable=True)
    back_order = jnp.argsort(slot_token)
    slot_place = jnp.argsort(back_order)

    def pack_home(rows_in):
        return jnp.take(rows_in, send_order, axis=0)

    def place_window(rows_in):
        return jnp.take(rows_in, slot_place, axis=0)

    both = jnp.concatenate([tokens, cotangent], axis=0).transpose(1, 0, 2)
    both = both.reshape(row_count, -1)
    both = place_window(
        lax.all_to_all(pack_home(both), "tok", split_axis=0, concat_axis=0, tiled=True)
    )
    both = both.reshape(row_count, 2 * micro_count, feature_width).transpose(1, 0, 2)
    tokens, cotangent = both[:micro_count], both[micro_count:]
    steps_total = micro_count + section_count - 1
    zero_rows = jnp.zeros((micro_count, row_count, feature_width), jnp.bfloat16)
    start_carry = (
        jnp.zeros((row_count, feature_width), jnp.bfloat16),
        zero_rows,
        zero_rows,
        zero_rows,
        jnp.zeros((micro_count, row_count, 3 * feature_width), jnp.bfloat16),
    )

    def forward_step(step_index, carried):
        inflow, kept_input, kept_normed, kept_mixed, kept_window = carried
        micro_index = step_index - section_index
        active = (micro_index >= 0) & (micro_index < micro_count)
        clipped = jnp.clip(micro_index, 0, micro_count - 1)
        entering = lax.dynamic_index_in_dim(
            tokens, jnp.clip(step_index, 0, micro_count - 1), 0, keepdims=False
        )
        layer_in = jnp.where(section_index == 0, entering, inflow)
        normed = normalize(layer_in, norm_scale)[0]
        projected = jnp.dot(normed, qkv_matrix, preferred_element_type=jnp.float32).astype(
            jnp.bfloat16
        )
        window_rows = projected
        mixed_rows = window_forward(window_rows)
        layer_out = (
            layer_in.astype(jnp.float32)
            + jnp.dot(mixed_rows, out_matrix, preferred_element_type=jnp.float32)
        ).astype(jnp.bfloat16)
        kept_input = stored_update(kept_input, clipped, active, layer_in)
        kept_normed = stored_update(kept_normed, clipped, active, normed)
        kept_mixed = stored_update(kept_mixed, clipped, active, mixed_rows)
        kept_window = stored_update(kept_window, clipped, active, window_rows)
        outflow = from_behind(layer_out, "section", 1)
        return (outflow, kept_input, kept_normed, kept_mixed, kept_window)

    leftover, kept_input, kept_normed, kept_mixed, kept_window = lax.fori_loop(
        0, steps_total, forward_step, start_carry
    )

    def backward_step(step_index, carried):
        inflow, qkv_total, out_total, scale_total = carried
        micro_index = step_index - (section_count - 1 - section_index)
        active = (micro_index >= 0) & (micro_index < micro_count)
        weight_on = active.astype(jnp.float32)
        clipped = jnp.clip(micro_index, 0, micro_count - 1)
        arriving = lax.dynamic_index_in_dim(
            cotangent, jnp.clip(step_index, 0, micro_count - 1), 0, keepdims=False
        )
        grad_layer = jnp.where(section_index == section_count - 1, arriving, inflow)
        layer_in = lax.dynamic_index_in_dim(kept_input, clipped, 0, keepdims=False)
        kept_rows = lax.dynamic_index_in_dim(kept_normed, clipped, 0, keepdims=False)
        mixed_rows = lax.dynamic_index_in_dim(kept_mixed, clipped, 0, keepdims=False)
        window_rows = lax.dynamic_index_in_dim(kept_window, clipped, 0, keepdims=False)
        out_total = out_total + weight_on * jnp.einsum(
            "td,te->de", mixed_rows, grad_layer, preferred_element_type=jnp.float32
        )
        grad_mixed = jnp.einsum(
            "te,de->td", grad_layer, out_matrix, preferred_element_type=jnp.float32
        ).astype(jnp.bfloat16)
        grad_proj = window_backward(window_rows, grad_mixed)
        qkv_total = qkv_total + weight_on * jnp.einsum(
            "td,tc->dc", kept_rows, grad_proj, preferred_element_type=jnp.float32
        )
        grad_normed = jnp.einsum(
            "tc,dc->td", grad_proj, qkv_matrix, preferred_element_type=jnp.float32
        )
        widened = layer_in.astype(jnp.float32)
        factor = lax.rsqrt(jnp.mean(widened * widened, axis=-1, keepdims=True) + EPSILON)
        scale_total = scale_total + weight_on * jnp.sum(grad_normed * widened * factor, axis=0)
        scaled = norm_scale * grad_normed
        inner_mean = jnp.mean(scaled * widened, axis=-1, keepdims=True)
        grad_input = (
            grad_layer.astype(jnp.float32) + factor * scaled - widened * factor**3 * inner_mean
        ).astype(jnp.bfloat16)
        outflow = from_behind(grad_input, "section", -1)
        return (outflow, qkv_total, out_total, scale_total)

    back_carry = (
        jnp.zeros((row_count, feature_width), jnp.bfloat16),
        jnp.zeros(qkv_matrix.shape, jnp.float32),
        jnp.zeros(out_matrix.shape, jnp.float32),
        jnp.zeros(norm_scale.shape, jnp.float32),
    )
    leftover_grad, qkv_total, out_total, scale_total = lax.fori_loop(
        0, steps_total, backward_step, back_carry
    )
    qkv_share, out_share, scale_share = (
        lax.psum_scatter(qkv_total, "tok", scatter_dimension=0, tiled=True),
        lax.psum_scatter(out_total, "tok", scatter_dimension=0, tiled=True),
        lax.psum_scatter(scale_total, "tok", scatter_dimension=0, tiled=True),
    )
    return (qkv_share[None], out_share[None], scale_share[None])


def solution(mesh):
    placed = (
        P(None, "tok", None),
        P(None, "tok", None),
        P("tok"),
        P("tok"),
        P("section", None),
        P("section", None, None),
        P("section", None, None),
    )
    return jax.shard_map(
        per_device,
        mesh=mesh,
        in_specs=placed,
        out_specs=(P("section", "tok", None), P("section", "tok", None), P("section", "tok")),
        check_vma=False,
    )
```

```python
import functools

import jax
import jax.numpy as jnp
from jax import lax
from jax.experimental import pallas as pl
from jax.experimental.pallas import tpu as pltpu
from jax.sharding import PartitionSpec as P

HEADS = 12
WINDOW = 32
PAIR = 128
EPSILON = 1e-06
F32 = jnp.float32
BF16 = jnp.bfloat16


def dot_nn(a, b):
    return lax.dot_general(a, b, (((1,), (0,)), ((), ())), preferred_element_type=F32)


def dot_nt(a, b):
    return lax.dot_general(a, b, (((1,), (1,)), ((), ())), preferred_element_type=F32)


def dot_tn(a, b):
    return lax.dot_general(a, b, (((0,), (0,)), ((), ())), preferred_element_type=F32)


def to_section(src, dst, send, recv, section):
    return pltpu.make_async_remote_copy(
        src_ref=src,
        dst_ref=dst,
        send_sem=send,
        recv_sem=recv,
        device_id={"section": section},
        device_id_type=pl.DeviceIdType.MESH,
    )


def chain_kernel(
    sections, micros, enter_ref, gain_ref, wqkv_ref, wout_ref,
    dqkv_ref, dout_ref, dgain_ref,
    x_keep, g_keep, n_keep, a_keep, qkv_keep, p_keep, dp_keep, xbox, gbox,
    fwd_send, fwd_recv, bwd_send, bwd_recv,
):
    rows, width = enter_ref.shape[1], enter_ref.shape[2]
    head_dim = width // HEADS
    temper = head_dim ** (-0.5)
    here = lax.axis_index("section")
    first, last = here == 0, here == sections - 1
    barrier = pltpu.get_barrier_semaphore()

    @pl.when(jnp.logical_not(first))
    def _():
        pl.semaphore_signal(barrier, inc=1, device_id={"section": here - 1},
                            device_id_type=pl.DeviceIdType.MESH)

    @pl.when(jnp.logical_not(last))
    def _():
        pl.semaphore_signal(barrier, inc=1, device_id={"section": here + 1},
                            device_id_type=pl.DeviceIdType.MESH)

    middle = jnp.logical_not(jnp.logical_or(first, last))

    @pl.when(middle)
    def _():
        pl.semaphore_wait(barrier, 2)

    @pl.when(jnp.logical_not(middle))
    def _():
        pl.semaphore_wait(barrier, 1)

    gain = gain_ref[...]
    lane = lax.broadcasted_iota(jnp.int32, (1, PAIR), 1)
    low = jnp.where(lane < head_dim, 1.0, 0.0).astype(BF16)
    high = jnp.where(lane < head_dim, 0.0, 1.0).astype(BF16)
    row_window = lax.broadcasted_iota(jnp.int32, (rows, rows), 0) // WINDOW
    col_window = lax.broadcasted_iota(jnp.int32, (rows, rows), 1) // WINDOW
    hide = jnp.where(row_window == col_window, 0.0, -1e30)
    hide = jnp.concatenate([hide, hide], axis=0)

    def two(value):
        return jnp.concatenate([value * low, value * high], axis=0)

    def beside(value):
        return jnp.concatenate([value[:rows], value[rows:]], axis=1)

    def fwd_copy(m):
        return to_section(xbox.at[m], x_keep.at[m], fwd_send.at[m], fwd_recv.at[m], here + 1)

    def bwd_copy(m):
        return to_section(gbox.at[m], g_keep.at[m], bwd_send.at[m], bwd_recv.at[m], here - 1)

    def factor_of(x):
        return lax.rsqrt(jnp.mean(x * x, axis=-1, keepdims=True) + EPSILON)

    for m in range(micros):
        span = slice(m * rows, (m + 1) * rows)

        @pl.when(first)
        def _():
            x_keep[m] = enter_ref[m]

        @pl.when(jnp.logical_not(first))
        def _():
            fwd_copy(m).wait_recv()

        x = x_keep[m].astype(F32)
        normed = (x * factor_of(x) * gain).astype(BF16)
        n_keep[span, :] = normed
        for c in range(0, 3 * width, 256):
            qkv_keep[m, :, c:c + 256] = dot_nn(normed, wqkv_ref[:, c:c + 256]).astype(BF16)
        for j in range(width // PAIR):
            c = j * PAIR
            q = qkv_keep[m, :, c:c + PAIR]
            k = qkv_keep[m, :, width + c:width + c + PAIR]
            v = qkv_keep[m, :, 2 * width + c:2 * width + c + PAIR]
            scores = dot_nt(two(q), k) * temper + hide
            top = jnp.max(scores, axis=-1, keepdims=True)
            raised = jnp.exp(scores - top)
            soft = raised / jnp.sum(raised, axis=-1, keepdims=True)
            p_keep[m, j] = soft
            mixed = dot_nn(beside(soft.astype(BF16)), two(v))
            a_keep[span, c:c + PAIR] = mixed.astype(BF16)

        @pl.when(jnp.logical_not(last))
        def _():
            xbox[m] = (x_keep[m].astype(F32) + dot_nn(a_keep[span, :], wout_ref[...])).astype(BF16)
            fwd_copy(m).start()

    for m in range(micros):
        span = slice(m * rows, (m + 1) * rows)

        @pl.when(last)
        def _():
            g_keep[m] = enter_ref[micros + m]

        @pl.when(jnp.logical_not(last))
        def _():
            bwd_copy(m).wait_recv()

        grad_mixed = dot_nt(g_keep[m], wout_ref[...]).astype(BF16)
        for j in range(width // PAIR):
            c = j * PAIR
            q = qkv_keep[m, :, c:c + PAIR]
            k = qkv_keep[m, :, width + c:width + c + PAIR]
            v = qkv_keep[m, :, 2 * width + c:2 * width + c + PAIR]
            dw = two(grad_mixed[:, c:c + PAIR])
            soft = p_keep[m, j]
            grad_soft = dot_nt(dw, v)
            grad_scores = soft * (grad_soft - jnp.sum(soft * grad_soft, axis=-1, keepdims=True))
            low_scores = grad_scores.astype(BF16)
            dq = dot_nn(beside(low_scores), two(k)) * temper
            dk = dot_tn(low_scores, two(q)) * temper
            dv = dot_tn(soft.astype(BF16), dw)
            dp_keep[span, c:c + PAIR] = dq.astype(BF16)
            dp_keep[span, width + c:width + c + PAIR] = dk.astype(BF16)
            dp_keep[span, 2 * width + c:2 * width + c + PAIR] = dv.astype(BF16)
        grad_normed = dot_nt(dp_keep[span, :], wqkv_ref[...])
        x = x_keep[m].astype(F32)
        factor = factor_of(x)

        @pl.when(jnp.logical_not(first))
        def _():
            scaled = gain * grad_normed
            inner = jnp.mean(scaled * x, axis=-1, keepdims=True)
            gbox[m] = (g_keep[m].astype(F32) + factor * scaled - x * (factor * factor * factor) * inner).astype(BF16)
            bwd_copy(m).start()

        piece = jnp.sum(grad_normed * x * factor, axis=0, keepdims=True)
        if m == 0:
            dgain_ref[...] = piece
        else:
            dgain_ref[...] += piece

    g_all = g_keep[...].reshape(micros * rows, width)
    for c in range(0, width, 256):
        dout_ref[:, c:c + 256] = dot_tn(a_keep[...], g_all[:, c:c + 256])
    for c in range(0, 3 * width, 256):
        dqkv_ref[:, c:c + 256] = dot_tn(n_keep[...], dp_keep[:, c:c + 256])

    for m in range(micros):
        @pl.when(jnp.logical_not(last))
        def _():
            fwd_copy(m).wait_send()

        @pl.when(jnp.logical_not(first))
        def _():
            bwd_copy(m).wait_send()


def per_device(tokens, cotangent, window_slot, slot_token, norm_gain, qkv_weight, out_weight):
    micros, rows, width = tokens.shape
    sections = lax.axis_size("section")
    send_order = jnp.argsort(window_slot // rows, stable=True)
    slot_place = jnp.argsort(jnp.argsort(slot_token))
    both = jnp.concatenate([tokens, cotangent], axis=0).transpose(1, 0, 2).reshape(rows, -1)
    both = lax.all_to_all(
        jnp.take(both, send_order, axis=0), "tok", split_axis=0, concat_axis=0, tiled=True
    )
    both = jnp.take(both, slot_place, axis=0)
    enter = both.reshape(rows, 2 * micros, width).transpose(1, 0, 2)
    in_vmem = pl.BlockSpec(memory_space=pltpu.VMEM)
    dma = pltpu.SemaphoreType.DMA((micros,))
    qkv_total, out_total, gain_total = pl.pallas_call(
        functools.partial(chain_kernel, sections, micros),
        out_shape=(
            jax.ShapeDtypeStruct((width, 3 * width), F32),
            jax.ShapeDtypeStruct((width, width), F32),
            jax.ShapeDtypeStruct((1, width), F32),
        ),
        in_specs=[in_vmem] * 4,
        out_specs=[in_vmem] * 3,
        scratch_shapes=[
            pltpu.VMEM((micros, rows, width), BF16),
            pltpu.VMEM((micros, rows, width), BF16),
            pltpu.VMEM((micros * rows, width), BF16),
            pltpu.VMEM((micros * rows, width), BF16),
            pltpu.VMEM((micros, rows, 3 * width), BF16),
            pltpu.VMEM((micros, width // PAIR, 2 * rows, rows), F32),
            pltpu.VMEM((micros * rows, 3 * width), BF16),
            pltpu.VMEM((micros, rows, width), BF16),
            pltpu.VMEM((micros, rows, width), BF16),
            dma, dma, dma, dma,
        ],
        compiler_params=pltpu.CompilerParams(
            collective_id=0, has_side_effects=True, vmem_limit_bytes=50 * 2**20
        ),
        name="chain",
    )(enter, norm_gain, qkv_weight[0], out_weight[0])
    qkv_share = lax.psum_scatter(qkv_total, "tok", scatter_dimension=0, tiled=True)
    out_share = lax.psum_scatter(out_total, "tok", scatter_dimension=0, tiled=True)
    gain_share = lax.psum_scatter(gain_total[0], "tok", scatter_dimension=0, tiled=True)
    return (qkv_share[None], out_share[None], gain_share[None])


def solution(mesh):
    placed = (
        P(None, "tok", None),
        P(None, "tok", None),
        P("tok"),
        P("tok"),
        P("section", None),
        P("section", None, None),
        P("section", None, None),
    )
    return jax.shard_map(
        per_device,
        mesh=mesh,
        in_specs=placed,
        out_specs=(P("section", "tok", None), P("section", "tok", None), P("section", "tok")),
        check_vma=False,
    )
```

```python
import functools

import jax
import jax.numpy as jnp
from jax import lax
from jax.experimental import pallas as pl
from jax.experimental.pallas import tpu as pltpu
from jax.sharding import PartitionSpec as P

HEADS = 12
WINDOW = 32
PAIR = 128
EPSILON = 1e-06
F32 = jnp.float32
BF16 = jnp.bfloat16


def dot_nn(a, b):
    return lax.dot_general(a, b, (((1,), (0,)), ((), ())), preferred_element_type=F32)


def dot_nt(a, b):
    return lax.dot_general(a, b, (((1,), (1,)), ((), ())), preferred_element_type=F32)


def dot_tn(a, b):
    return lax.dot_general(a, b, (((0,), (0,)), ((), ())), preferred_element_type=F32)


def to_section(src, dst, send, recv, section):
    return pltpu.make_async_remote_copy(
        src_ref=src,
        dst_ref=dst,
        send_sem=send,
        recv_sem=recv,
        device_id={"section": section},
        device_id_type=pl.DeviceIdType.MESH,
    )


def chain_kernel(
    sections, toks, micros, reduce_here, enter_ref, gain_ref, wqkv_ref, wout_ref,
    dqkv_ref, dout_ref, dgain_ref,
    x_keep, g_keep, n_keep, a_keep, qkv_keep, p_keep, dp_keep, xbox, gbox,
    fwd_send, fwd_recv, bwd_send, bwd_recv, *reduce_refs,
):
    rows, width = enter_ref.shape[1], enter_ref.shape[2]
    head_dim = width // HEADS
    temper = head_dim ** (-0.5)
    here = lax.axis_index("section")
    first, last = here == 0, here == sections - 1
    barrier = pltpu.get_barrier_semaphore()

    def greet(condition, **peer):
        @pl.when(condition)
        def _():
            pl.semaphore_signal(barrier, inc=1, device_id=peer,
                                device_id_type=pl.DeviceIdType.MESH)

    greet(jnp.logical_not(first), section=here - 1)
    greet(jnp.logical_not(last), section=here + 1)
    peers = jnp.where(first, 0, 1) + jnp.where(last, 0, 1)
    if reduce_here:
        tok_at = lax.axis_index("tok")
        depth, core = tok_at // 2, tok_at % 2
        depths = toks // 2
        greet(depth > 0, tok=tok_at - 2)
        greet(depth < depths - 1, tok=tok_at + 2)
        greet(depth >= 0, tok=tok_at + 1 - 2 * core)
        peers = peers + 1 + jnp.where(depth > 0, 1, 0) + jnp.where(depth < depths - 1, 1, 0)
    pl.semaphore_wait(barrier, peers)

    gain = gain_ref[...]
    lane = lax.broadcasted_iota(jnp.int32, (1, PAIR), 1)
    low = jnp.where(lane < head_dim, 1.0, 0.0).astype(BF16)
    high = jnp.where(lane < head_dim, 0.0, 1.0).astype(BF16)
    row_window = lax.broadcasted_iota(jnp.int32, (rows, rows), 0) // WINDOW
    col_window = lax.broadcasted_iota(jnp.int32, (rows, rows), 1) // WINDOW
    hide = jnp.where(row_window == col_window, 0.0, -1e30)
    hide = jnp.concatenate([hide, hide], axis=0)

    def two(value):
        return jnp.concatenate([value * low, value * high], axis=0)

    def beside(value):
        return jnp.concatenate([value[:rows], value[rows:]], axis=1)

    def fwd_copy(m):
        return to_section(xbox.at[m], x_keep.at[m], fwd_send.at[m], fwd_recv.at[m], here + 1)

    def bwd_copy(m):
        return to_section(gbox.at[m], g_keep.at[m], bwd_send.at[m], bwd_recv.at[m], here - 1)

    def factor_of(x):
        return lax.rsqrt(jnp.mean(x * x, axis=-1, keepdims=True) + EPSILON)

    for m in range(micros):
        span = slice(m * rows, (m + 1) * rows)

        @pl.when(first)
        def _():
            x_keep[m] = enter_ref[m]

        @pl.when(jnp.logical_not(first))
        def _():
            fwd_copy(m).wait_recv()

        x = x_keep[m].astype(F32)
        normed = (x * factor_of(x) * gain).astype(BF16)
        n_keep[span, :] = normed
        for c in range(0, 3 * width, 256):
            qkv_keep[m, :, c:c + 256] = dot_nn(normed, wqkv_ref[:, c:c + 256]).astype(BF16)
        for j in range(width // PAIR):
            c = j * PAIR
            q = qkv_keep[m, :, c:c + PAIR]
            k = qkv_keep[m, :, width + c:width + c + PAIR]
            v = qkv_keep[m, :, 2 * width + c:2 * width + c + PAIR]
            scores = dot_nt(two(q), k) * temper + hide
            top = jnp.max(scores, axis=-1, keepdims=True)
            raised = jnp.exp(scores - top)
            soft = raised / jnp.sum(raised, axis=-1, keepdims=True)
            p_keep[m, j] = soft
            mixed = dot_nn(beside(soft.astype(BF16)), two(v))
            a_keep[span, c:c + PAIR] = mixed.astype(BF16)

        @pl.when(jnp.logical_not(last))
        def _():
            xbox[m] = (x_keep[m].astype(F32) + dot_nn(a_keep[span, :], wout_ref[...])).astype(BF16)
            fwd_copy(m).start()

    for m in range(micros):
        span = slice(m * rows, (m + 1) * rows)

        @pl.when(last)
        def _():
            g_keep[m] = enter_ref[micros + m]

        @pl.when(jnp.logical_not(last))
        def _():
            bwd_copy(m).wait_recv()

        grad_mixed = dot_nt(g_keep[m], wout_ref[...]).astype(BF16)
        for j in range(width // PAIR):
            c = j * PAIR
            q = qkv_keep[m, :, c:c + PAIR]
            k = qkv_keep[m, :, width + c:width + c + PAIR]
            v = qkv_keep[m, :, 2 * width + c:2 * width + c + PAIR]
            dw = two(grad_mixed[:, c:c + PAIR])
            soft = p_keep[m, j]
            grad_soft = dot_nt(dw, v)
            grad_scores = soft * (grad_soft - jnp.sum(soft * grad_soft, axis=-1, keepdims=True))
            low_scores = grad_scores.astype(BF16)
            dq = dot_nn(beside(low_scores), two(k)) * temper
            dk = dot_tn(low_scores, two(q)) * temper
            dv = dot_tn(soft.astype(BF16), dw)
            dp_keep[span, c:c + PAIR] = dq.astype(BF16)
            dp_keep[span, width + c:width + c + PAIR] = dk.astype(BF16)
            dp_keep[span, 2 * width + c:2 * width + c + PAIR] = dv.astype(BF16)
        grad_normed = dot_nt(dp_keep[span, :], wqkv_ref[...])
        x = x_keep[m].astype(F32)
        factor = factor_of(x)

        @pl.when(jnp.logical_not(first))
        def _():
            scaled = gain * grad_normed
            inner = jnp.mean(scaled * x, axis=-1, keepdims=True)
            gbox[m] = (g_keep[m].astype(F32) + factor * scaled - x * (factor * factor * factor) * inner).astype(BF16)
            bwd_copy(m).start()

        piece = jnp.sum(grad_normed * x * factor, axis=0, keepdims=True)
        gain_total = piece if m == 0 else gain_total + piece

    g_all = g_keep[...].reshape(micros * rows, width)
    if reduce_here:
        (total, core_send, core_recv, up_send, up_recv, down_send, down_recv,
         core_ss, core_rs, up_ss, up_rs, down_ss, down_rs) = reduce_refs
        total_qkv, total_out = total.at[:, :3 * width], total.at[:, 3 * width:4 * width]
        total[:, 4 * width:] = jnp.transpose(jnp.broadcast_to(gain_total, (PAIR, width)))
    else:
        total_qkv, total_out = dqkv_ref, dout_ref
        dgain_ref[...] = gain_total
    for c in range(0, width, 256):
        total_out[:, c:c + 256] = dot_tn(a_keep[...], g_all[:, c:c + 256])
    for c in range(0, 3 * width, 256):
        total_qkv[:, c:c + 256] = dot_tn(n_keep[...], dp_keep[:, c:c + 256])

    if reduce_here:
        share = width // toks
        order = []
        for i in range(depths):
            for d in (depths - 1 - i, i):
                if d not in order:
                    order.append(d)

        def part(d, c):
            return total[pl.ds(pl.multiple_of((2 * d + c) * share, share), share), :]

        def to_tok(src, dst, send, recv, tok):
            return pltpu.make_async_remote_copy(
                src_ref=src, dst_ref=dst, send_sem=send, recv_sem=recv,
                device_id={"tok": tok}, device_id_type=pl.DeviceIdType.MESH,
            )

        def core_copy(d):
            return to_tok(core_send.at[d], core_recv.at[d], core_ss.at[d], core_rs.at[d],
                          tok_at + 1 - 2 * core)

        def up_copy(d):
            return to_tok(up_send.at[d], up_recv.at[d], up_ss.at[d], up_rs.at[d], tok_at + 2)

        def down_copy(d):
            return to_tok(down_send.at[d], down_recv.at[d], down_ss.at[d], down_rs.at[d],
                          tok_at - 2)

        for d in order:
            core_send[d] = part(d, 1 - core).astype(BF16)
            core_copy(d).start()

        def pass_up(d):
            @pl.when(depth == 0)
            def _():
                up_send[d] = (part(d, core) + core_recv[d].astype(F32)).astype(BF16)

            @pl.when(depth > 0)
            def _():
                up_copy(d).wait_recv()
                up_send[d] = (part(d, core) + core_recv[d].astype(F32)
                              + up_recv[d].astype(F32)).astype(BF16)

            up_copy(d).start()

        def pass_down(d):
            @pl.when(depth == depths - 1)
            def _():
                down_send[d] = (part(d, core) + core_recv[d].astype(F32)).astype(BF16)

            @pl.when(depth < depths - 1)
            def _():
                down_copy(d).wait_recv()
                down_send[d] = (part(d, core) + core_recv[d].astype(F32)
                                + down_recv[d].astype(F32)).astype(BF16)

            down_copy(d).start()

        waited = []
        for i in range(depths):
            for d in (depths - 1 - i, i):
                if d not in waited:
                    core_copy(d).wait_recv()
                    waited.append(d)
            if i < depths - 1:
                pl.when(depth < depths - 1 - i)(functools.partial(pass_up, depths - 1 - i))
                pl.when(depth > i)(functools.partial(pass_down, i))

        for d in range(depths):
            @pl.when(depth == d)
            def _():
                mine = part(d, core) + core_recv[d].astype(F32)
                if d > 0:
                    up_copy(d).wait_recv()
                    mine = mine + up_recv[d].astype(F32)
                if d < depths - 1:
                    down_copy(d).wait_recv()
                    mine = mine + down_recv[d].astype(F32)
                dqkv_ref[...] = mine[:, :3 * width]
                dout_ref[...] = mine[:, 3 * width:4 * width]
                dgain_ref[...] = mine[:, 4 * width:]

            core_copy(d).wait_send()

            @pl.when(depth < d)
            def _():
                up_copy(d).wait_send()

            @pl.when(depth > d)
            def _():
                down_copy(d).wait_send()

    for m in range(micros):
        @pl.when(jnp.logical_not(last))
        def _():
            fwd_copy(m).wait_send()

        @pl.when(jnp.logical_not(first))
        def _():
            bwd_copy(m).wait_send()


def per_device(tokens, cotangent, window_slot, slot_token, norm_gain, qkv_weight, out_weight):
    micros, rows, width = tokens.shape
    sections = lax.axis_size("section")
    toks = lax.axis_size("tok")
    share = width // toks
    reduce_here = toks % 2 == 0 and toks >= 4 and share % 16 == 0 and width % toks == 0
    place = jnp.arange(rows, dtype=jnp.int32)
    target = (window_slot // rows) * rows + place
    send_rank = jnp.sum((target[None, :] < target[:, None]).astype(jnp.int32), axis=1)
    send_order = jnp.sum(jnp.where(send_rank[None, :] == place[:, None], place[None, :], 0), axis=1)
    slot_place = jnp.sum((slot_token[None, :] < slot_token[:, None]).astype(jnp.int32), axis=1)
    both = jnp.concatenate([tokens, cotangent], axis=0).transpose(1, 0, 2).reshape(rows, -1)
    both = lax.all_to_all(
        jnp.take(both, send_order, axis=0), "tok", split_axis=0, concat_axis=0, tiled=True
    )
    both = jnp.take(both, slot_place, axis=0)
    enter = both.reshape(rows, 2 * micros, width).transpose(1, 0, 2)
    in_vmem = pl.BlockSpec(memory_space=pltpu.VMEM)
    dma = pltpu.SemaphoreType.DMA((micros,))
    if reduce_here:
        out_shape = (
            jax.ShapeDtypeStruct((share, 3 * width), F32),
            jax.ShapeDtypeStruct((share, width), F32),
            jax.ShapeDtypeStruct((share, PAIR), F32),
        )
        box = pltpu.VMEM((toks // 2, share, 4 * width + PAIR), BF16)
        extra = [pltpu.VMEM((width, 4 * width + PAIR), F32)] + [box] * 6
        extra += [pltpu.SemaphoreType.DMA((toks // 2,))] * 6
    else:
        out_shape = (
            jax.ShapeDtypeStruct((width, 3 * width), F32),
            jax.ShapeDtypeStruct((width, width), F32),
            jax.ShapeDtypeStruct((1, width), F32),
        )
        extra = []
    qkv_total, out_total, gain_total = pl.pallas_call(
        functools.partial(chain_kernel, sections, toks, micros, reduce_here),
        out_shape=out_shape,
        in_specs=[in_vmem] * 4,
        out_specs=[in_vmem] * 3,
        scratch_shapes=[
            pltpu.VMEM((micros, rows, width), BF16),
            pltpu.VMEM((micros, rows, width), BF16),
            pltpu.VMEM((micros * rows, width), BF16),
            pltpu.VMEM((micros * rows, width), BF16),
            pltpu.VMEM((micros, rows, 3 * width), BF16),
            pltpu.VMEM((micros, width // PAIR, 2 * rows, rows), F32),
            pltpu.VMEM((micros * rows, 3 * width), BF16),
            pltpu.VMEM((micros, rows, width), BF16),
            pltpu.VMEM((micros, rows, width), BF16),
            dma, dma, dma, dma,
            *extra,
        ],
        compiler_params=pltpu.CompilerParams(
            collective_id=0, has_side_effects=True, vmem_limit_bytes=56 * 2**20
        ),
        name="chain",
    )(enter, norm_gain, qkv_weight[0], out_weight[0])
    if reduce_here:
        return (qkv_total[None], out_total[None], gain_total[:, 0][None])
    qkv_share = lax.psum_scatter(qkv_total, "tok", scatter_dimension=0, tiled=True)
    out_share = lax.psum_scatter(out_total, "tok", scatter_dimension=0, tiled=True)
    gain_share = lax.psum_scatter(gain_total[0], "tok", scatter_dimension=0, tiled=True)
    return (qkv_share[None], out_share[None], gain_share[None])


def solution(mesh):
    placed = (
        P(None, "tok", None),
        P(None, "tok", None),
        P("tok"),
        P("tok"),
        P("section", None),
        P("section", None, None),
        P("section", None, None),
    )
    return jax.shard_map(
        per_device,
        mesh=mesh,
        in_specs=placed,
        out_specs=(P("section", "tok", None), P("section", "tok", None), P("section", "tok")),
        check_vma=False,
    )
```

```python
import functools

import jax
import jax.numpy as jnp
from jax import lax
from jax.experimental import pallas as pl
from jax.experimental.pallas import tpu as pltpu
from jax.sharding import PartitionSpec as P

HEADS = 12
WINDOW = 32
PAIR = 128
EPSILON = 1e-06
F32 = jnp.float32
BF16 = jnp.bfloat16


def dot_nn(a, b):
    return lax.dot_general(a, b, (((1,), (0,)), ((), ())), preferred_element_type=F32)


def dot_nt(a, b):
    return lax.dot_general(a, b, (((1,), (1,)), ((), ())), preferred_element_type=F32)


def dot_tn(a, b):
    return lax.dot_general(a, b, (((0,), (0,)), ((), ())), preferred_element_type=F32)


def to_section(src, dst, send, recv, section):
    return pltpu.make_async_remote_copy(
        src_ref=src,
        dst_ref=dst,
        send_sem=send,
        recv_sem=recv,
        device_id={"section": section},
        device_id_type=pl.DeviceIdType.MESH,
    )


def chain_kernel(
    sections, toks, micros, reduce_here, enter_ref, leave_ref, send_ref, place_ref, gain_ref, wqkv_ref, wout_ref,
    dqkv_ref, dout_ref, dgain_ref,
    x_keep, g_keep, n_keep, a_keep, qkv_keep, p_keep, dp_keep, xbox, gbox,
    fwd_send, fwd_recv, bwd_send, bwd_recv, *reduce_refs,
):
    rows, width = enter_ref.shape[1], enter_ref.shape[2]
    share = width // toks
    head_dim = width // HEADS
    temper = head_dim ** (-0.5)
    here = lax.axis_index("section")
    first, last = here == 0, here == sections - 1
    barrier = pltpu.get_barrier_semaphore()

    def greet(condition, **peer):
        @pl.when(condition)
        def _():
            pl.semaphore_signal(barrier, inc=1, device_id=peer,
                                device_id_type=pl.DeviceIdType.MESH)

    greet(jnp.logical_not(first), section=here - 1)
    greet(jnp.logical_not(last), section=here + 1)
    peers = jnp.where(first, 0, 1) + jnp.where(last, 0, 1)
    if reduce_here:
        tok_at = lax.axis_index("tok")
        depth, core = tok_at // 2, tok_at % 2
        depths = toks // 2
        for o in range(1, toks):
            greet(depth >= 0, tok=(tok_at + o) % toks)
        peers = peers + (toks - 1)
    pl.semaphore_wait(barrier, peers)

    gain = gain_ref[...]
    lane = lax.broadcasted_iota(jnp.int32, (1, PAIR), 1)
    low = jnp.where(lane < head_dim, 1.0, 0.0).astype(BF16)
    high = jnp.where(lane < head_dim, 0.0, 1.0).astype(BF16)
    row_window = lax.broadcasted_iota(jnp.int32, (rows, rows), 0) // WINDOW
    col_window = lax.broadcasted_iota(jnp.int32, (rows, rows), 1) // WINDOW
    hide = jnp.where(row_window == col_window, 0.0, -1e30)
    hide = jnp.concatenate([hide, hide], axis=0)

    if reduce_here:
        (total, core_send, core_recv, up_send, up_recv, down_send, down_recv,
         core_ss, core_rs, up_ss, up_rs, down_ss, down_rs,
         packed, landed, packed_ss, packed_rs) = reduce_refs
        outer = jnp.logical_or(first, last)
        block = rows // toks

        def rows_of(index):
            return pl.ds(pl.multiple_of(index * block, block), block)

        def shuffle_copy(o):
            return pltpu.make_async_remote_copy(
                src_ref=packed.at[:, rows_of((tok_at + o) % toks), :],
                dst_ref=landed.at[:, rows_of(tok_at), :],
                send_sem=packed_ss.at[o], recv_sem=packed_rs.at[o],
                device_id={"tok": (tok_at + o) % toks}, device_id_type=pl.DeviceIdType.MESH,
            )

        def pack(source_ref):
            spot = lax.broadcasted_iota(jnp.int32, (rows, rows), 0)
            pick = jnp.where(spot == send_ref[...], 1.0, 0.0).astype(BF16)
            for m in range(micros):
                packed[m] = dot_nn(pick, source_ref[m]).astype(BF16)

        def unpack(target_ref):
            spot = lax.broadcasted_iota(jnp.int32, (rows, rows), 1)
            pick = jnp.where(spot == place_ref[...], 1.0, 0.0).astype(BF16)
            for m in range(micros):
                target_ref[m] = dot_nn(pick, landed[m]).astype(BF16)

        pl.when(first)(lambda: pack(enter_ref))
        pl.when(last)(lambda: pack(leave_ref))

        @pl.when(outer)
        def _():
            for o in range(1, toks):
                shuffle_copy(o).start()
            landed[:, rows_of(tok_at), :] = packed[:, rows_of(tok_at), :]
            for o in range(1, toks):
                shuffle_copy(o).wait()

        pl.when(first)(lambda: unpack(x_keep))
        pl.when(last)(lambda: unpack(g_keep))

    def two(value):
        return jnp.concatenate([value * low, value * high], axis=0)

    def beside(value):
        return jnp.concatenate([value[:rows], value[rows:]], axis=1)

    def fwd_copy(m):
        return to_section(xbox.at[m], x_keep.at[m], fwd_send.at[m], fwd_recv.at[m], here + 1)

    def bwd_copy(m):
        return to_section(gbox.at[m], g_keep.at[m], bwd_send.at[m], bwd_recv.at[m], here - 1)

    def factor_of(x):
        return lax.rsqrt(jnp.mean(x * x, axis=-1, keepdims=True) + EPSILON)

    for m in range(micros):
        span = slice(m * rows, (m + 1) * rows)

        if not reduce_here:
            @pl.when(first)
            def _():
                x_keep[m] = enter_ref[m]

        @pl.when(jnp.logical_not(first))
        def _():
            fwd_copy(m).wait_recv()

        x = x_keep[m].astype(F32)
        normed = (x * factor_of(x) * gain).astype(BF16)
        n_keep[span, :] = normed
        for c in range(0, 3 * width, 256):
            qkv_keep[m, :, c:c + 256] = dot_nn(normed, wqkv_ref[:, c:c + 256]).astype(BF16)
        for j in range(width // PAIR):
            c = j * PAIR
            q = qkv_keep[m, :, c:c + PAIR]
            k = qkv_keep[m, :, width + c:width + c + PAIR]
            v = qkv_keep[m, :, 2 * width + c:2 * width + c + PAIR]
            scores = dot_nt(two(q), k) * temper + hide
            top = jnp.max(scores, axis=-1, keepdims=True)
            raised = jnp.exp(scores - top)
            soft = raised / jnp.sum(raised, axis=-1, keepdims=True)
            p_keep[m, j] = soft
            mixed = dot_nn(beside(soft.astype(BF16)), two(v))
            a_keep[span, c:c + PAIR] = mixed.astype(BF16)

        @pl.when(jnp.logical_not(last))
        def _():
            xbox[m] = (x_keep[m].astype(F32) + dot_nn(a_keep[span, :], wout_ref[...])).astype(BF16)
            fwd_copy(m).start()

    for m in range(micros):
        span = slice(m * rows, (m + 1) * rows)

        if not reduce_here:
            @pl.when(last)
            def _():
                g_keep[m] = leave_ref[m]

        @pl.when(jnp.logical_not(last))
        def _():
            bwd_copy(m).wait_recv()

        grad_mixed = dot_nt(g_keep[m], wout_ref[...]).astype(BF16)
        for j in range(width // PAIR):
            c = j * PAIR
            q = qkv_keep[m, :, c:c + PAIR]
            k = qkv_keep[m, :, width + c:width + c + PAIR]
            v = qkv_keep[m, :, 2 * width + c:2 * width + c + PAIR]
            dw = two(grad_mixed[:, c:c + PAIR])
            soft = p_keep[m, j]
            grad_soft = dot_nt(dw, v)
            grad_scores = soft * (grad_soft - jnp.sum(soft * grad_soft, axis=-1, keepdims=True))
            low_scores = grad_scores.astype(BF16)
            dq = dot_nn(beside(low_scores), two(k)) * temper
            dk = dot_tn(low_scores, two(q)) * temper
            dv = dot_tn(soft.astype(BF16), dw)
            dp_keep[span, c:c + PAIR] = dq.astype(BF16)
            dp_keep[span, width + c:width + c + PAIR] = dk.astype(BF16)
            dp_keep[span, 2 * width + c:2 * width + c + PAIR] = dv.astype(BF16)
        grad_normed = dot_nt(dp_keep[span, :], wqkv_ref[...])
        x = x_keep[m].astype(F32)
        factor = factor_of(x)

        @pl.when(jnp.logical_not(first))
        def _():
            scaled = gain * grad_normed
            inner = jnp.mean(scaled * x, axis=-1, keepdims=True)
            gbox[m] = (g_keep[m].astype(F32) + factor * scaled - x * (factor * factor * factor) * inner).astype(BF16)
            bwd_copy(m).start()

        piece = jnp.sum(grad_normed * x * factor, axis=0, keepdims=True)
        gain_total = piece if m == 0 else gain_total + piece

    g_all = g_keep[...].reshape(micros * rows, width)
    if reduce_here:
        total_qkv, total_out = total.at[:, :3 * width], total.at[:, 3 * width:4 * width]
        total[:, 4 * width:] = jnp.transpose(jnp.broadcast_to(gain_total, (PAIR, width)))
    else:
        total_qkv, total_out = dqkv_ref, dout_ref
        dgain_ref[...] = gain_total
    for c in range(0, width, 256):
        total_out[:, c:c + 256] = dot_tn(a_keep[...], g_all[:, c:c + 256])
    for c in range(0, 3 * width, 256):
        total_qkv[:, c:c + 256] = dot_tn(n_keep[...], dp_keep[:, c:c + 256])

    if reduce_here:
        order = []
        for i in range(depths):
            for d in (depths - 1 - i, i):
                if d not in order:
                    order.append(d)

        def part(d, c):
            return total[pl.ds(pl.multiple_of((2 * d + c) * share, share), share), :]

        def to_tok(src, dst, send, recv, tok):
            return pltpu.make_async_remote_copy(
                src_ref=src, dst_ref=dst, send_sem=send, recv_sem=recv,
                device_id={"tok": tok}, device_id_type=pl.DeviceIdType.MESH,
            )

        def core_copy(d):
            return to_tok(core_send.at[d], core_recv.at[d], core_ss.at[d], core_rs.at[d],
                          tok_at + 1 - 2 * core)

        def up_copy(d):
            return to_tok(up_send.at[d], up_recv.at[d], up_ss.at[d], up_rs.at[d], tok_at + 2)

        def down_copy(d):
            return to_tok(down_send.at[d], down_recv.at[d], down_ss.at[d], down_rs.at[d],
                          tok_at - 2)

        for d in order:
            core_send[d] = part(d, 1 - core).astype(BF16)
            core_copy(d).start()

        def pass_up(d):
            @pl.when(depth == 0)
            def _():
                up_send[d] = (part(d, core) + core_recv[d].astype(F32)).astype(BF16)

            @pl.when(depth > 0)
            def _():
                up_copy(d).wait_recv()
                up_send[d] = (part(d, core) + core_recv[d].astype(F32)
                              + up_recv[d].astype(F32)).astype(BF16)

            up_copy(d).start()

        def pass_down(d):
            @pl.when(depth == depths - 1)
            def _():
                down_send[d] = (part(d, core) + core_recv[d].astype(F32)).astype(BF16)

            @pl.when(depth < depths - 1)
            def _():
                down_copy(d).wait_recv()
                down_send[d] = (part(d, core) + core_recv[d].astype(F32)
                                + down_recv[d].astype(F32)).astype(BF16)

            down_copy(d).start()

        waited = []
        for i in range(depths):
            for d in (depths - 1 - i, i):
                if d not in waited:
                    core_copy(d).wait_recv()
                    waited.append(d)
            if i < depths - 1:
                pl.when(depth < depths - 1 - i)(functools.partial(pass_up, depths - 1 - i))
                pl.when(depth > i)(functools.partial(pass_down, i))

        for d in range(depths):
            @pl.when(depth == d)
            def _():
                mine = part(d, core) + core_recv[d].astype(F32)
                if d > 0:
                    up_copy(d).wait_recv()
                    mine = mine + up_recv[d].astype(F32)
                if d < depths - 1:
                    down_copy(d).wait_recv()
                    mine = mine + down_recv[d].astype(F32)
                dqkv_ref[...] = mine[:, :3 * width]
                dout_ref[...] = mine[:, 3 * width:4 * width]
                dgain_ref[...] = mine[:, 4 * width:]

            core_copy(d).wait_send()

            @pl.when(depth < d)
            def _():
                up_copy(d).wait_send()

            @pl.when(depth > d)
            def _():
                down_copy(d).wait_send()

    for m in range(micros):
        @pl.when(jnp.logical_not(last))
        def _():
            fwd_copy(m).wait_send()

        @pl.when(jnp.logical_not(first))
        def _():
            bwd_copy(m).wait_send()


def per_device(tokens, cotangent, window_slot, slot_token, norm_gain, qkv_weight, out_weight):
    micros, rows, width = tokens.shape
    sections = lax.axis_size("section")
    toks = lax.axis_size("tok")
    share = width // toks
    reduce_here = toks % 2 == 0 and toks >= 4 and share % 16 == 0 and width % toks == 0
    reduce_here = reduce_here and rows % (16 * toks) == 0
    place = jnp.arange(rows, dtype=jnp.int32)
    target = (window_slot // rows) * rows + place
    send_rank = jnp.sum((target[None, :] < target[:, None]).astype(jnp.int32), axis=1)
    slot_place = jnp.sum((slot_token[None, :] < slot_token[:, None]).astype(jnp.int32), axis=1)
    enter, leave = tokens, cotangent
    if not reduce_here:
        send_order = jnp.sum(
            jnp.where(send_rank[None, :] == place[:, None], place[None, :], 0), axis=1
        )
        both = jnp.concatenate([tokens, cotangent], axis=0).transpose(1, 0, 2).reshape(rows, -1)
        both = lax.all_to_all(
            jnp.take(both, send_order, axis=0), "tok", split_axis=0, concat_axis=0, tiled=True
        )
        both = jnp.take(both, slot_place, axis=0)
        both = both.reshape(rows, 2 * micros, width).transpose(1, 0, 2)
        enter, leave = both[:micros], both[micros:]
    in_vmem = pl.BlockSpec(memory_space=pltpu.VMEM)
    dma = pltpu.SemaphoreType.DMA((micros,))
    if reduce_here:
        out_shape = (
            jax.ShapeDtypeStruct((share, 3 * width), F32),
            jax.ShapeDtypeStruct((share, width), F32),
            jax.ShapeDtypeStruct((share, PAIR), F32),
        )
        box = pltpu.VMEM((toks // 2, share, 4 * width + PAIR), BF16)
        extra = [pltpu.VMEM((width, 4 * width + PAIR), F32)] + [box] * 6
        extra += [pltpu.SemaphoreType.DMA((toks // 2,))] * 6
        extra += [pltpu.VMEM((micros, rows, width), BF16)] * 2
        extra += [pltpu.SemaphoreType.DMA((toks,))] * 2
    else:
        out_shape = (
            jax.ShapeDtypeStruct((width, 3 * width), F32),
            jax.ShapeDtypeStruct((width, width), F32),
            jax.ShapeDtypeStruct((1, width), F32),
        )
        extra = []
    qkv_total, out_total, gain_total = pl.pallas_call(
        functools.partial(chain_kernel, sections, toks, micros, reduce_here),
        out_shape=out_shape,
        in_specs=[in_vmem] * 7,
        out_specs=[in_vmem] * 3,
        scratch_shapes=[
            pltpu.VMEM((micros, rows, width), BF16),
            pltpu.VMEM((micros, rows, width), BF16),
            pltpu.VMEM((micros * rows, width), BF16),
            pltpu.VMEM((micros * rows, width), BF16),
            pltpu.VMEM((micros, rows, 3 * width), BF16),
            pltpu.VMEM((micros, width // PAIR, 2 * rows, rows), F32),
            pltpu.VMEM((micros * rows, 3 * width), BF16),
            pltpu.VMEM((micros, rows, width), BF16),
            pltpu.VMEM((micros, rows, width), BF16),
            dma, dma, dma, dma,
            *extra,
        ],
        compiler_params=pltpu.CompilerParams(
            collective_id=0, has_side_effects=True, vmem_limit_bytes=56 * 2**20
        ),
        name="chain",
    )(enter, leave, send_rank[None], slot_place[:, None], norm_gain, qkv_weight[0], out_weight[0])
    if reduce_here:
        return (qkv_total[None], out_total[None], gain_total[:, 0][None])
    qkv_share = lax.psum_scatter(qkv_total, "tok", scatter_dimension=0, tiled=True)
    out_share = lax.psum_scatter(out_total, "tok", scatter_dimension=0, tiled=True)
    gain_share = lax.psum_scatter(gain_total[0], "tok", scatter_dimension=0, tiled=True)
    return (qkv_share[None], out_share[None], gain_share[None])


def solution(mesh):
    placed = (
        P(None, "tok", None),
        P(None, "tok", None),
        P("tok"),
        P("tok"),
        P("section", None),
        P("section", None, None),
        P("section", None, None),
    )
    return jax.shard_map(
        per_device,
        mesh=mesh,
        in_specs=placed,
        out_specs=(P("section", "tok", None), P("section", "tok", None), P("section", "tok")),
        check_vma=False,
    )
```

```python
import functools

import jax
import jax.numpy as jnp
from jax import lax
from jax.experimental import pallas as pl
from jax.experimental.pallas import tpu as pltpu
from jax.sharding import PartitionSpec as P

HEADS = 12
WINDOW = 32
PAIR = 128
EPSILON = 1e-06
F32 = jnp.float32
BF16 = jnp.bfloat16


def dot_nn(a, b):
    return lax.dot_general(a, b, (((1,), (0,)), ((), ())), preferred_element_type=F32)


def dot_nt(a, b):
    return lax.dot_general(a, b, (((1,), (1,)), ((), ())), preferred_element_type=F32)


def dot_tn(a, b):
    return lax.dot_general(a, b, (((0,), (0,)), ((), ())), preferred_element_type=F32)


def to_section(src, dst, send, recv, section):
    return pltpu.make_async_remote_copy(
        src_ref=src,
        dst_ref=dst,
        send_sem=send,
        recv_sem=recv,
        device_id={"section": section},
        device_id_type=pl.DeviceIdType.MESH,
    )


def chain_kernel(
    sections, toks, micros, reduce_here, enter_ref, leave_ref, send_ref, place_ref, gain_ref, wqkv_ref, wout_ref,
    dqkv_ref, dout_ref, dgain_ref,
    x_keep, g_keep, n_keep, a_keep, qkv_keep, p_keep, dp_keep, xbox, gbox,
    fwd_send, fwd_recv, bwd_send, bwd_recv, *reduce_refs,
):
    rows, width = enter_ref.shape[1], enter_ref.shape[2]
    share = width // toks
    head_dim = width // HEADS
    temper = head_dim ** (-0.5)
    here = lax.axis_index("section")
    first, last = here == 0, here == sections - 1
    barrier = pltpu.get_barrier_semaphore()

    def greet(condition, **peer):
        @pl.when(condition)
        def _():
            pl.semaphore_signal(barrier, inc=1, device_id=peer,
                                device_id_type=pl.DeviceIdType.MESH)

    greet(jnp.logical_not(first), section=here - 1)
    greet(jnp.logical_not(last), section=here + 1)
    peers = jnp.where(first, 0, 1) + jnp.where(last, 0, 1)
    if reduce_here:
        tok_at = lax.axis_index("tok")
        depth, core = tok_at // 2, tok_at % 2
        depths = toks // 2
        for o in range(1, toks):
            greet(depth >= 0, tok=(tok_at + o) % toks)
        peers = peers + (toks - 1)
    pl.semaphore_wait(barrier, peers)

    gain = gain_ref[...]
    lane = lax.broadcasted_iota(jnp.int32, (1, PAIR), 1)
    low = jnp.where(lane < head_dim, 1.0, 0.0).astype(BF16)
    high = jnp.where(lane < head_dim, 0.0, 1.0).astype(BF16)
    row_window = lax.broadcasted_iota(jnp.int32, (rows, rows), 0) // WINDOW
    col_window = lax.broadcasted_iota(jnp.int32, (rows, rows), 1) // WINDOW
    hide = jnp.where(row_window == col_window, 0.0, -1e30)
    hide = jnp.concatenate([hide, hide], axis=0)

    if reduce_here:
        (total, core_send, core_recv, up_send, up_recv, down_send, down_recv,
         core_ss, core_rs, up_ss, up_rs, down_ss, down_rs,
         packed, landed, packed_ss, packed_rs) = reduce_refs
        outer = jnp.logical_or(first, last)
        block = rows // toks

        def rows_of(index):
            return pl.ds(pl.multiple_of(index * block, block), block)

        def shuffle_copy(o):
            return pltpu.make_async_remote_copy(
                src_ref=packed.at[:, rows_of((tok_at + o) % toks), :],
                dst_ref=landed.at[:, rows_of(tok_at), :],
                send_sem=packed_ss.at[o], recv_sem=packed_rs.at[o],
                device_id={"tok": (tok_at + o) % toks}, device_id_type=pl.DeviceIdType.MESH,
            )

        def pack(source_ref):
            spot = lax.broadcasted_iota(jnp.int32, (rows, rows), 0)
            pick = jnp.where(spot == send_ref[...], 1.0, 0.0).astype(BF16)
            for m in range(micros):
                packed[m] = dot_nn(pick, source_ref[m]).astype(BF16)

        def unpack(target_ref):
            spot = lax.broadcasted_iota(jnp.int32, (rows, rows), 1)
            pick = jnp.where(spot == place_ref[...], 1.0, 0.0).astype(BF16)
            for m in range(micros):
                target_ref[m] = dot_nn(pick, landed[m]).astype(BF16)

        pl.when(first)(lambda: pack(enter_ref))
        pl.when(last)(lambda: pack(leave_ref))

        @pl.when(outer)
        def _():
            for o in range(1, toks):
                shuffle_copy(o).start()
            landed[:, rows_of(tok_at), :] = packed[:, rows_of(tok_at), :]
            for o in range(1, toks):
                shuffle_copy(o).wait_recv()

        pl.when(first)(lambda: unpack(x_keep))
        pl.when(last)(lambda: unpack(g_keep))

    def two(value):
        return jnp.concatenate([value * low, value * high], axis=0)

    def beside(value):
        return jnp.concatenate([value[:rows], value[rows:]], axis=1)

    def fwd_copy(m):
        return to_section(xbox.at[m], x_keep.at[m], fwd_send.at[m], fwd_recv.at[m], here + 1)

    def bwd_copy(m):
        return to_section(gbox.at[m], g_keep.at[m], bwd_send.at[m], bwd_recv.at[m], here - 1)

    def factor_of(x):
        return lax.rsqrt(jnp.mean(x * x, axis=-1, keepdims=True) + EPSILON)

    for m in range(micros):
        span = slice(m * rows, (m + 1) * rows)

        if not reduce_here:
            @pl.when(first)
            def _():
                x_keep[m] = enter_ref[m]

        @pl.when(jnp.logical_not(first))
        def _():
            fwd_copy(m).wait_recv()

        x = x_keep[m].astype(F32)
        normed = (x * factor_of(x) * gain).astype(BF16)
        n_keep[span, :] = normed
        for c in range(0, 3 * width, 256):
            qkv_keep[m, :, c:c + 256] = dot_nn(normed, wqkv_ref[:, c:c + 256]).astype(BF16)
        for j in range(width // PAIR):
            c = j * PAIR
            q = qkv_keep[m, :, c:c + PAIR]
            k = qkv_keep[m, :, width + c:width + c + PAIR]
            v = qkv_keep[m, :, 2 * width + c:2 * width + c + PAIR]
            scores = dot_nt(two(q), k) * temper + hide
            top = jnp.max(scores, axis=-1, keepdims=True)
            raised = jnp.exp(scores - top)
            soft = raised * (1.0 / jnp.sum(raised, axis=-1, keepdims=True))
            p_keep[m, j] = soft
            mixed = dot_nn(beside(soft.astype(BF16)), two(v))
            a_keep[span, c:c + PAIR] = mixed.astype(BF16)

        @pl.when(jnp.logical_not(last))
        def _():
            xbox[m] = (x_keep[m].astype(F32) + dot_nn(a_keep[span, :], wout_ref[...])).astype(BF16)
            fwd_copy(m).start()

    for m in range(micros):
        span = slice(m * rows, (m + 1) * rows)

        if not reduce_here:
            @pl.when(last)
            def _():
                g_keep[m] = leave_ref[m]

        @pl.when(jnp.logical_not(last))
        def _():
            bwd_copy(m).wait_recv()

        grad_mixed = dot_nt(g_keep[m], wout_ref[...]).astype(BF16)
        for j in range(width // PAIR):
            c = j * PAIR
            q = qkv_keep[m, :, c:c + PAIR]
            k = qkv_keep[m, :, width + c:width + c + PAIR]
            v = qkv_keep[m, :, 2 * width + c:2 * width + c + PAIR]
            dw = two(grad_mixed[:, c:c + PAIR])
            soft = p_keep[m, j]
            grad_soft = dot_nt(dw, v)
            grad_scores = soft * (grad_soft - jnp.sum(soft * grad_soft, axis=-1, keepdims=True))
            low_scores = grad_scores.astype(BF16)
            dq = dot_nn(beside(low_scores), two(k)) * temper
            dk = dot_tn(low_scores, two(q)) * temper
            dv = dot_tn(soft.astype(BF16), dw)
            dp_keep[span, c:c + PAIR] = dq.astype(BF16)
            dp_keep[span, width + c:width + c + PAIR] = dk.astype(BF16)
            dp_keep[span, 2 * width + c:2 * width + c + PAIR] = dv.astype(BF16)
        grad_normed = dot_nt(dp_keep[span, :], wqkv_ref[...])
        x = x_keep[m].astype(F32)
        factor = factor_of(x)

        @pl.when(jnp.logical_not(first))
        def _():
            scaled = gain * grad_normed
            inner = jnp.mean(scaled * x, axis=-1, keepdims=True)
            gbox[m] = (g_keep[m].astype(F32) + factor * scaled - x * (factor * factor * factor) * inner).astype(BF16)
            bwd_copy(m).start()

        piece = jnp.sum(grad_normed * x * factor, axis=0, keepdims=True)
        gain_total = piece if m == 0 else gain_total + piece

    g_all = g_keep[...].reshape(micros * rows, width)
    if reduce_here:
        total_qkv, total_out = total.at[:, :3 * width], total.at[:, 3 * width:4 * width]
        total[:, 4 * width:] = jnp.transpose(jnp.broadcast_to(gain_total, (PAIR, width)))
    else:
        total_qkv, total_out = dqkv_ref, dout_ref
        dgain_ref[...] = gain_total
    for c in range(0, width, 256):
        total_out[:, c:c + 256] = dot_tn(a_keep[...], g_all[:, c:c + 256])
    for c in range(0, 3 * width, 256):
        total_qkv[:, c:c + 256] = dot_tn(n_keep[...], dp_keep[:, c:c + 256])

    if reduce_here:
        order = []
        for i in range(depths):
            for d in (depths - 1 - i, i):
                if d not in order:
                    order.append(d)

        def part(d, c):
            return total[pl.ds(pl.multiple_of((2 * d + c) * share, share), share), :]

        def to_tok(src, dst, send, recv, tok):
            return pltpu.make_async_remote_copy(
                src_ref=src, dst_ref=dst, send_sem=send, recv_sem=recv,
                device_id={"tok": tok}, device_id_type=pl.DeviceIdType.MESH,
            )

        def core_copy(d):
            return to_tok(core_send.at[d], core_recv.at[d], core_ss.at[d], core_rs.at[d],
                          tok_at + 1 - 2 * core)

        def up_copy(d):
            return to_tok(up_send.at[d], up_recv.at[d], up_ss.at[d], up_rs.at[d], tok_at + 2)

        def down_copy(d):
            return to_tok(down_send.at[d], down_recv.at[d], down_ss.at[d], down_rs.at[d],
                          tok_at - 2)

        for d in order:
            core_send[d] = part(d, 1 - core).astype(BF16)
            core_copy(d).start()

        def pass_up(d):
            @pl.when(depth == 0)
            def _():
                up_send[d] = (part(d, core) + core_recv[d].astype(F32)).astype(BF16)

            @pl.when(depth > 0)
            def _():
                up_copy(d).wait_recv()
                up_send[d] = (part(d, core) + core_recv[d].astype(F32)
                              + up_recv[d].astype(F32)).astype(BF16)

            up_copy(d).start()

        def pass_down(d):
            @pl.when(depth == depths - 1)
            def _():
                down_send[d] = (part(d, core) + core_recv[d].astype(F32)).astype(BF16)

            @pl.when(depth < depths - 1)
            def _():
                down_copy(d).wait_recv()
                down_send[d] = (part(d, core) + core_recv[d].astype(F32)
                                + down_recv[d].astype(F32)).astype(BF16)

            down_copy(d).start()

        waited = []
        for i in range(depths):
            for d in (depths - 1 - i, i):
                if d not in waited:
                    core_copy(d).wait_recv()
                    waited.append(d)
            if i < depths - 1:
                pl.when(depth < depths - 1 - i)(functools.partial(pass_up, depths - 1 - i))
                pl.when(depth > i)(functools.partial(pass_down, i))

        for d in range(depths):
            @pl.when(depth == d)
            def _():
                mine = part(d, core) + core_recv[d].astype(F32)
                if d > 0:
                    up_copy(d).wait_recv()
                    mine = mine + up_recv[d].astype(F32)
                if d < depths - 1:
                    down_copy(d).wait_recv()
                    mine = mine + down_recv[d].astype(F32)
                dqkv_ref[...] = mine[:, :3 * width]
                dout_ref[...] = mine[:, 3 * width:4 * width]
                dgain_ref[...] = mine[:, 4 * width:]

            core_copy(d).wait_send()

            @pl.when(depth < d)
            def _():
                up_copy(d).wait_send()

            @pl.when(depth > d)
            def _():
                down_copy(d).wait_send()

    if reduce_here:
        @pl.when(outer)
        def _():
            for o in range(1, toks):
                shuffle_copy(o).wait_send()

    for m in range(micros):
        @pl.when(jnp.logical_not(last))
        def _():
            fwd_copy(m).wait_send()

        @pl.when(jnp.logical_not(first))
        def _():
            bwd_copy(m).wait_send()


def per_device(tokens, cotangent, window_slot, slot_token, norm_gain, qkv_weight, out_weight):
    micros, rows, width = tokens.shape
    sections = lax.axis_size("section")
    toks = lax.axis_size("tok")
    share = width // toks
    reduce_here = toks % 2 == 0 and toks >= 4 and share % 16 == 0 and width % toks == 0
    reduce_here = reduce_here and rows % (16 * toks) == 0
    place = jnp.arange(rows, dtype=jnp.int32)
    target = (window_slot // rows) * rows + place
    send_rank = jnp.sum((target[None, :] < target[:, None]).astype(jnp.int32), axis=1)
    slot_place = jnp.sum((slot_token[None, :] < slot_token[:, None]).astype(jnp.int32), axis=1)
    enter, leave = tokens, cotangent
    if not reduce_here:
        send_order = jnp.sum(
            jnp.where(send_rank[None, :] == place[:, None], place[None, :], 0), axis=1
        )
        both = jnp.concatenate([tokens, cotangent], axis=0).transpose(1, 0, 2).reshape(rows, -1)
        both = lax.all_to_all(
            jnp.take(both, send_order, axis=0), "tok", split_axis=0, concat_axis=0, tiled=True
        )
        both = jnp.take(both, slot_place, axis=0)
        both = both.reshape(rows, 2 * micros, width).transpose(1, 0, 2)
        enter, leave = both[:micros], both[micros:]
    in_vmem = pl.BlockSpec(memory_space=pltpu.VMEM)
    dma = pltpu.SemaphoreType.DMA((micros,))
    if reduce_here:
        out_shape = (
            jax.ShapeDtypeStruct((share, 3 * width), F32),
            jax.ShapeDtypeStruct((share, width), F32),
            jax.ShapeDtypeStruct((share, PAIR), F32),
        )
        box = pltpu.VMEM((toks // 2, share, 4 * width + PAIR), BF16)
        extra = [pltpu.VMEM((width, 4 * width + PAIR), F32)] + [box] * 6
        extra += [pltpu.SemaphoreType.DMA((toks // 2,))] * 6
        extra += [pltpu.VMEM((micros, rows, width), BF16)] * 2
        extra += [pltpu.SemaphoreType.DMA((toks,))] * 2
    else:
        out_shape = (
            jax.ShapeDtypeStruct((width, 3 * width), F32),
            jax.ShapeDtypeStruct((width, width), F32),
            jax.ShapeDtypeStruct((1, width), F32),
        )
        extra = []
    qkv_total, out_total, gain_total = pl.pallas_call(
        functools.partial(chain_kernel, sections, toks, micros, reduce_here),
        out_shape=out_shape,
        in_specs=[in_vmem] * 7,
        out_specs=[in_vmem] * 3,
        scratch_shapes=[
            pltpu.VMEM((micros, rows, width), BF16),
            pltpu.VMEM((micros, rows, width), BF16),
            pltpu.VMEM((micros * rows, width), BF16),
            pltpu.VMEM((micros * rows, width), BF16),
            pltpu.VMEM((micros, rows, 3 * width), BF16),
            pltpu.VMEM((micros, width // PAIR, 2 * rows, rows), F32),
            pltpu.VMEM((micros * rows, 3 * width), BF16),
            pltpu.VMEM((micros, rows, width), BF16),
            pltpu.VMEM((micros, rows, width), BF16),
            dma, dma, dma, dma,
            *extra,
        ],
        compiler_params=pltpu.CompilerParams(
            collective_id=0, has_side_effects=True, vmem_limit_bytes=56 * 2**20
        ),
        name="chain",
    )(enter, leave, send_rank[None], slot_place[:, None], norm_gain, qkv_weight[0], out_weight[0])
    if reduce_here:
        return (qkv_total[None], out_total[None], gain_total[:, 0][None])
    qkv_share = lax.psum_scatter(qkv_total, "tok", scatter_dimension=0, tiled=True)
    out_share = lax.psum_scatter(out_total, "tok", scatter_dimension=0, tiled=True)
    gain_share = lax.psum_scatter(gain_total[0], "tok", scatter_dimension=0, tiled=True)
    return (qkv_share[None], out_share[None], gain_share[None])


def solution(mesh):
    placed = (
        P(None, "tok", None),
        P(None, "tok", None),
        P("tok"),
        P("tok"),
        P("section", None),
        P("section", None, None),
        P("section", None, None),
    )
    return jax.shard_map(
        per_device,
        mesh=mesh,
        in_specs=placed,
        out_specs=(P("section", "tok", None), P("section", "tok", None), P("section", "tok")),
        check_vma=False,
    )
```
